32 devices in a mesh: section: 4 (over x, core), seq: 2 (over y), dp: 4 (over z).
Axes of the slice: x: 2, y: 2, z: 4, core: 2. Of those that a mesh axis runs over, the one named last changes fastest.
Arguments:
- act_rows: bfloat16 [4, 4, 128, 4096], P('section', 'dp', 'seq'), may hold values from -30 to 30
- mem_rows: bfloat16 [4, 4, 128, 4096], P('section', 'dp', 'seq'), may hold values from -30 to 30
- w_query: bfloat16 [4, 4096, 4096], P('section', 'dp', 'seq'), may hold values from -8 to 8
- w_key: bfloat16 [4, 4096, 4096], P('section', 'dp', 'seq'), may hold values from -8 to 8
- w_value: bfloat16 [4, 4096, 4096], P('section', 'dp', 'seq'), may hold values from -0.09375 to 0.09375
- w_out: bfloat16 [4, 4096, 4096], P('section', ('seq', 'dp')), may hold values from -0.09375 to 0.09375
- ln_gain: float32 [4, 4096], P('section'), may hold values from 0.5 to 1.5
- final_gain: float32 [4096], replicated, may hold values from 0.5 to 1.5
- src_len: int32 [4, 4], P('section', 'dp'), may hold values from 32 to 128
- tgt_len: int32 [4, 4], P('section', 'dp'), may hold values from 32 to 128
Outputs:
- act_next: bfloat16 [4, 4, 128, 4096], P('section', 'dp', 'seq')
- mem_next: bfloat16 [4, 4, 128, 4096], P('section', 'dp', 'seq')
The draws below stay inside these ranges and needn't reach their ends.
All inputs are finite; a program needn't handle non-finite values.
Results may differ from the reference program's by a relative error of at most 0.013.
The reference program's roundings to bfloat16 on the way count: a program that leaves them out, or rounds other values in their place, can miss the bound.
Values may be sent and summed in bfloat16 or wider, within the bound.
A program may use at most 128 MiB of HBM per device.

```python
import math
import jax
import jax.numpy as jnp
from jax import lax

D = 4096
HEADS = 64
HEAD_DIM = 64
SEQ_LEN = 128
SEQS = 4
SECTIONS = 4
N_SEQ = 2


def row_scales(key, shape):
    return jnp.exp(jax.random.uniform(key, shape, jnp.float32, math.log(0.3), math.log(3.0)))


def memory_base(key):
    shape = (SECTIONS, SEQS, SEQ_LEN, D)
    return jnp.clip(jax.random.normal(jax.random.fold_in(key, 201), shape, jnp.float32), -5.0, 5.0)


def draw_mem_rows(key, part):
    values = memory_base(key) * row_scales(jax.random.fold_in(key, 211), (SECTIONS, SEQS, SEQ_LEN, 1))
    return values.astype(jnp.bfloat16)


def draw_act_rows(key, part):
    shape = (SECTIONS, SEQS, SEQ_LEN, D)
    own_part = jnp.clip(jax.random.normal(jax.random.fold_in(key, 202), shape, jnp.float32), -5.0, 5.0)
    values = own_part * row_scales(jax.random.fold_in(key, 212), (SECTIONS, SEQS, SEQ_LEN, 1))
    return values.astype(jnp.bfloat16)


def query_base(key):
    shape = (SECTIONS, D, HEADS * HEAD_DIM)
    return jnp.clip(jax.random.normal(jax.random.fold_in(key, 301), shape, jnp.float32), -6.0, 6.0)


def draw_w_query(key, part):
    values = query_base(key) * (1.0 / math.sqrt(D))
    return values.astype(jnp.bfloat16)


def draw_w_key(key, part):
    shape = (SECTIONS, D, HEADS * HEAD_DIM)
    own_part = jnp.clip(jax.random.normal(jax.random.fold_in(key, 302), shape, jnp.float32), -6.0, 6.0)
    values = own_part * (1.0 / math.sqrt(D))
    return values.astype(jnp.bfloat16)


def with_ends(array, key, smallest, high):
    index_at = [jax.random.randint(jax.random.fold_in(key, axis), (), 0, length) for axis, length in enumerate(array.shape)]
    main_axis = array.shape.index(max(array.shape))
    neighbour = index_at[:main_axis] + [(index_at[main_axis] + 1) % array.shape[main_axis]] + index_at[main_axis + 1:]
    return array.at[tuple(index_at)].set(smallest).at[tuple(neighbour)].set(high)


def block_scale(stream_key, extent, cuts, least, high):
    level, own = 1.0, jax.random.fold_in(stream_key, 6)
    for dim, shards_of in cuts:
        heights = jnp.exp(jax.random.uniform(jax.random.fold_in(own, dim), (shards_of,), jnp.float32, least / len(cuts), high / len(cuts)))
        level = level * jnp.repeat(heights, extent[dim] // shards_of).reshape([-1 if axis == dim else 1 for axis in range(len(extent))])
    return level


def normal_values(rng, dims, spread, bound, shards=(), held_as=jnp.bfloat16):
    loudness = block_scale(rng, dims, shards, -0.22, 0.18) if shards else 1.0
    result = jax.random.normal(rng, dims, jnp.float32) * spread * loudness
    return jnp.minimum(jnp.maximum(result, -bound), bound).astype(held_as)


def setup_inputs(seed: int = 0) -> dict:
    seeds = jax.random.split(jax.random.key(seed), 11)
    act_rows = draw_act_rows(jax.random.fold_in(seeds[10], 71), 0)
    mem_rows = draw_mem_rows(jax.random.fold_in(seeds[10], 71), 0)
    w_query = draw_w_query(jax.random.fold_in(seeds[10], 71), 0)
    w_key = draw_w_key(jax.random.fold_in(seeds[10], 71), 0)
    w_value = normal_values(seeds[4], (SECTIONS, D, HEADS * HEAD_DIM), D ** -0.5, 0.09375, ((0, 4), (1, 4), (2, 2)))
    w_out = normal_values(seeds[5], (SECTIONS, HEADS * HEAD_DIM, D), (HEADS * HEAD_DIM) ** -0.5, 0.09375, ((0, 4), (1, 8)))
    ln_gain = jnp.clip(1.0 + 0.1 * jax.random.normal(seeds[6], (SECTIONS, D), jnp.float32), 0.5, 1.5)
    final_gain = jnp.clip(1.0 + 0.1 * jax.random.normal(seeds[7], (D,), jnp.float32), 0.5, 1.5)
    src_len = with_ends(jax.random.randint(seeds[8], (SECTIONS, SEQS), SEQ_LEN // 4, SEQ_LEN + 1), jax.random.fold_in(seeds[8], 1), SEQ_LEN // 4, SEQ_LEN).astype(jnp.int32)
    tgt_len = with_ends(jax.random.randint(seeds[9], (SECTIONS, SEQS), SEQ_LEN // 4, SEQ_LEN + 1), jax.random.fold_in(seeds[9], 1), SEQ_LEN // 4, SEQ_LEN).astype(jnp.int32)
    return {"act_rows": act_rows, "mem_rows": mem_rows, "w_query": w_query, "w_key": w_key, "w_value": w_value, "w_out": w_out, "ln_gain": ln_gain, "final_gain": final_gain, "src_len": src_len, "tgt_len": tgt_len}


EPS = 1e-06

def normed(rows, gain):
    values = rows.astype(jnp.float32)
    scaled = values * lax.rsqrt(lax.optimization_barrier(jnp.mean(values * values, axis=-1, keepdims=True)) + EPS)
    return (scaled * gain).astype(jnp.bfloat16)

def attend(query, key, value, src_length):
    total_rows = query.shape[0]
    query_heads = query.astype(jnp.float32).reshape(total_rows, HEADS, HEAD_DIM)
    key_heads = key.astype(jnp.float32).reshape(total_rows, HEADS, HEAD_DIM)
    value_heads = value.astype(jnp.float32).reshape(total_rows, HEADS, HEAD_DIM)
    scores = jnp.einsum('qhd,khd->hqk', query_heads, key_heads) * HEAD_DIM ** (-0.5)
    visible = jnp.arange(total_rows, dtype=jnp.int32) < src_length
    scores = jnp.where(visible[None, None, :], scores, -1e+30)
    top_score = lax.optimization_barrier(jnp.max(scores, axis=-1, keepdims=True))
    raw_weights = jnp.exp(scores - top_score)
    weights = (raw_weights / lax.optimization_barrier(jnp.sum(raw_weights, axis=-1, keepdims=True))).astype(jnp.bfloat16)
    heads_out = jnp.einsum('hqk,khd->qhd', weights.astype(jnp.float32), value_heads)
    return heads_out.astype(jnp.bfloat16).reshape(total_rows, HEADS * HEAD_DIM)

def reference(act_rows, mem_rows, w_query, w_key, w_value, w_out, ln_gain, final_gain, src_len, tgt_len):
    width = HEADS * HEAD_DIM
    group_cols = width // N_SEQ
    emit_act = []
    emit_mem = []
    for section in range(SECTIONS):
        act_list = []
        mem_list = []
        for sequence in range(SEQS):
            if section == 0:
                rows_in = mem_rows[0, sequence]
            else:
                rows_in = act_rows[section, sequence]
            residual = rows_in.astype(jnp.float32)
            query_in = normed(rows_in, ln_gain[section])
            if section == 0:
                source_in = query_in
            else:
                source_in = mem_rows[section, sequence]
            query = jnp.dot(query_in, w_query[section], preferred_element_type=jnp.float32).astype(jnp.bfloat16)
            key = jnp.dot(source_in, w_key[section], preferred_element_type=jnp.float32).astype(jnp.bfloat16)
            value = jnp.dot(source_in, w_value[section], preferred_element_type=jnp.float32).astype(jnp.bfloat16)
            heads_out = attend(query, key, value, src_len[section, sequence])
            update = jnp.zeros((SEQ_LEN, D), jnp.float32)
            for group in range(N_SEQ):
                low = group * group_cols
                high = low + group_cols
                partial_sum = jnp.dot(heads_out[:, low:high], w_out[section, low:high, :], preferred_element_type=jnp.float32).astype(jnp.bfloat16)
                partial_sum = lax.optimization_barrier(partial_sum)
                update = update + partial_sum.astype(jnp.float32)
            if section == 0:
                encoded = normed(residual + update, final_gain)
                act_list.append(act_rows[0, sequence])
                mem_list.append(encoded)
            else:
                positions = jnp.arange(SEQ_LEN, dtype=jnp.int32)
                keep_rows = (positions < tgt_len[section, sequence])[:, None]
                decoded = (residual + jnp.where(keep_rows, update, jnp.float32(0.0))).astype(jnp.bfloat16)
                act_list.append(decoded)
                mem_list.append(mem_rows[section, sequence])
        emit_act.append(jnp.stack(act_list))
        emit_mem.append(jnp.stack(mem_list))
    order = [SECTIONS - 1] + list(range(SECTIONS - 1))
    act_next = jnp.stack([emit_act[k] for k in order])
    mem_next = jnp.stack([emit_mem[k] for k in order])
    return (act_next, mem_next)
```

```python
import functools

import jax
import jax.numpy as jnp
from jax import lax
from jax.experimental import pallas as pl
from jax.experimental.pallas import tpu as pltpu
from jax.sharding import PartitionSpec as P

HEAD_DIM = 64


EPS = 1e-06


def passed_along(x, axis, by):
    count = lax.axis_size(axis)
    return lax.ppermute(x, axis, [(i, (i + by) % count) for i in range(count)])


def normed(rows, gain):
    values = rows.astype(jnp.float32)
    scaled = values * lax.rsqrt(jnp.mean(values * values, axis=-1, keepdims=True) + EPS)
    return (scaled * gain).astype(jnp.bfloat16)


def attend(queries, keys, values, src_len):
    seqs, total_rows, width = queries.shape
    head_count = width // HEAD_DIM
    shape = (seqs, total_rows, head_count, HEAD_DIM)
    queries, keys, values = (a.reshape(shape) for a in (queries, keys, values))
    visible = jnp.arange(total_rows, dtype=jnp.int32)[None, :] < src_len[:, None]
    scores = jnp.einsum(
        "bqhd,bkhd->bhqk", queries, keys, preferred_element_type=jnp.float32
    ) * HEAD_DIM ** (-0.5)
    scores = jnp.where(visible[:, None, None, :], scores, -1e30)
    top_score = jnp.max(scores, axis=-1, keepdims=True)
    raw_weights = jnp.exp(scores - top_score)
    weights = (raw_weights / jnp.sum(raw_weights, axis=-1, keepdims=True)).astype(jnp.bfloat16)
    heads = jnp.einsum("bhqk,bkhd->bqhd", weights, values, preferred_element_type=jnp.float32)
    return heads.astype(jnp.bfloat16).reshape(seqs, total_rows, width)


def per_device(
    act_rows, mem_rows, w_query, w_key, w_value, w_out, ln_gain, final_gain, src_len, tgt_len
):
    is_first = lax.axis_index("section") == 0
    seqs = lax.axis_size("dp")
    halves = lax.axis_size("seq")
    act_here = act_rows[0, 0]
    mem_here = mem_rows[0, 0]
    rows_here, width = act_here.shape
    gain = ln_gain[0]
    depth, cols = w_query.shape[1:]
    own = cols // seqs
    rows_in = jnp.where(is_first, mem_here, act_here)
    query_in = normed(rows_in, gain)
    source_in = jnp.where(is_first, query_in, mem_here)
    both = jnp.stack([query_in, source_in]).reshape(2, rows_here, seqs, depth)
    both = lax.all_to_all(both.transpose(2, 0, 1, 3), "dp", 0, 0, tiled=True)
    both = lax.all_gather(both, "seq", axis=0, tiled=False)
    both = both.transpose(2, 1, 0, 3, 4).reshape(2, seqs * halves * rows_here, depth)
    total = seqs * halves * rows_here

    def project(rows, weight):
        part = jnp.dot(rows, weight[0], preferred_element_type=jnp.float32).astype(jnp.bfloat16)
        part = part.reshape(total, seqs, own).transpose(1, 0, 2)
        part = lax.psum_scatter(part, "dp", scatter_dimension=0, tiled=False)
        return part.reshape(seqs, halves * rows_here, own)

    queries = project(both[0], w_query)
    keys = project(both[1], w_key)
    values = project(both[1], w_value)
    lengths = lax.all_gather(src_len[0], "dp", axis=0, tiled=True)
    heads_out = attend(queries, keys, values, lengths)
    update = jnp.dot(
        heads_out.reshape(total, own), w_out[0], preferred_element_type=jnp.float32
    ).astype(jnp.bfloat16).reshape(seqs, halves, rows_here, width)
    update = lax.psum_scatter(update, "seq", scatter_dimension=1, tiled=False)
    update = lax.psum_scatter(update, "dp", scatter_dimension=0, tiled=False).astype(jnp.float32)
    residual = rows_in.astype(jnp.float32)
    positions = lax.axis_index("seq") * rows_here + jnp.arange(rows_here, dtype=jnp.int32)
    keep_rows = (positions < tgt_len[0, 0])[:, None]
    decoded = (residual + jnp.where(keep_rows, update, jnp.float32(0.0))).astype(jnp.bfloat16)
    encoded = normed(residual + update, final_gain)
    emit_act = jnp.where(is_first, act_here, decoded)
    emit_mem = jnp.where(is_first, encoded, mem_here)
    next_act, next_mem = passed_along((emit_act, emit_mem), "section", 1)
    return (next_act[None, None], next_mem[None, None])


ROW_BLOCK = 16
LANES = 128
AHEAD = 2
OUT_CHUNK = 1024
VMEM_BYTES = 60 * 1024 * 1024
BF16 = jnp.bfloat16
F32 = jnp.float32


def scratch_of(seqs, rows, width, depth, cols):
    own, tokens = cols // seqs, 2 * rows
    vmem = {
        "weights": ((3, depth, cols), BF16),
        "w_out": ((own, width), BF16),
        "cut": ((2, seqs, rows, depth), BF16),
        "x": ((2, seqs, 2, rows, depth), BF16),
        "bias": ((seqs, 8, tokens), F32),
        "other": ((rows, width), BF16),
        "part": ((seqs, seqs, 3, tokens, own), BF16),
        "mine": ((seqs, 3, tokens, own), F32),
        "got": ((seqs, seqs - 1, 3, tokens, own), BF16),
        "qkv": ((3, tokens, own), BF16),
        "heads": ((tokens, own), BF16),
        "half": ((seqs, rows, width), F32),
        "y_out": ((seqs, rows, width), BF16),
        "y_in": ((seqs, rows, width), BF16),
        "z_out": ((seqs, rows, width), BF16),
        "z_in": ((seqs, rows, width), BF16),
        "late": ((rows, width), BF16),
    }
    sems = {
        "load": (4,),
        "cut_s": (2, seqs), "cut_r": (2, seqs),
        "fwd_s": (2, seqs), "fwd_r": (2, seqs),
        "bias_s": (seqs,), "bias_r": (seqs,),
        "part_s": (seqs, seqs - 1), "part_r": (seqs, seqs - 1),
        "y_s": (seqs,), "y_r": (seqs,),
        "z_s": (seqs,), "z_r": (seqs,),
        "hand_s": (2,), "hand_r": (2,),
    }
    return vmem, sems


def fits(seqs, halves, rows, width, depth, cols):
    own = cols // seqs
    if halves != 2 or rows % ROW_BLOCK or own % LANES or depth % LANES or width % OUT_CHUNK:
        return False
    vmem, _ = scratch_of(seqs, rows, width, depth, cols)
    total = 8 * rows * width * 2
    for shape, dtype in vmem.values():
        count = jnp.dtype(dtype).itemsize
        for extent in shape:
            count *= extent
        total += count
    return total <= VMEM_BYTES - 2 * 1024 * 1024


def tick_kernel(
    names, act, mem, w_q, w_k, w_v, w_o, gain, last_gain, src_len, tgt_len, early_out, late_out, *scratch
):
    refs = dict(zip(names, scratch))
    weights, w_out, cut, x, bias = (refs[n] for n in ("weights", "w_out", "cut", "x", "bias"))
    seqs, rows, depth = cut.shape[1:]
    width = act.shape[1]
    tokens = 2 * rows
    own = w_out.shape[0]
    sections = lax.axis_size("section")
    section = lax.axis_index("section")
    side = lax.axis_index("seq")
    me = lax.axis_index("dp")
    is_first = section == 0
    ahead = lax.rem(section + 1, sections)
    behind = lax.rem(section + sections - 1, sections)

    def remote(source, target, send, recv, device):
        return pltpu.make_async_remote_copy(
            src_ref=source, dst_ref=target, send_sem=send, recv_sem=recv,
            device_id=device, device_id_type=pl.DeviceIdType.MESH,
        )

    barrier = pltpu.get_barrier_semaphore()
    for step in range(1, seqs):
        pl.semaphore_signal(
            barrier, inc=1, device_id={"dp": lax.rem(me + step, seqs)},
            device_id_type=pl.DeviceIdType.MESH,
        )
    for device in ({"seq": 1 - side}, {"section": ahead}, {"section": behind}):
        pl.semaphore_signal(barrier, inc=1, device_id=device, device_id_type=pl.DeviceIdType.MESH)

    loads = [
        pltpu.make_async_copy(w_q, weights.at[0], refs["load"].at[0]),
        pltpu.make_async_copy(w_k, weights.at[1], refs["load"].at[1]),
        pltpu.make_async_copy(w_v, weights.at[2], refs["load"].at[2]),
        pltpu.make_async_copy(w_o, w_out, refs["load"].at[3]),
    ]
    for load in loads:
        load.start()

    def residual_rows(at):
        return jnp.where(is_first, mem[at, :], act[at, :]).astype(F32)

    def norm_block(r, carry):
        at = pl.ds(pl.multiple_of(r * ROW_BLOCK, ROW_BLOCK), ROW_BLOCK)
        query_in = normed(residual_rows(at), gain[...])
        source_in = jnp.where(is_first, query_in, mem[at, :])
        refs["other"][at, :] = jnp.where(is_first, act[at, :], mem[at, :])
        for j in range(seqs):
            cut[0, j, at, :] = query_in[:, j * depth:(j + 1) * depth]
            cut[1, j, at, :] = source_in[:, j * depth:(j + 1) * depth]
        return carry

    lax.fori_loop(0, rows // ROW_BLOCK, norm_block, 0)
    place = lax.broadcasted_iota(jnp.int32, (8, tokens), 1)
    bias[me] = jnp.where(place < src_len[0, 0], jnp.float32(0.0), jnp.float32(-1e30))
    pl.semaphore_wait(barrier, seqs + 2)

    def cut_copy(kind, to):
        return remote(
            cut.at[kind, to], x.at[kind, me, side], refs["cut_s"].at[kind, to],
            refs["cut_r"].at[kind, me], {"dp": to},
        )

    def bias_copy(to):
        return remote(
            bias.at[me], bias.at[me], refs["bias_s"].at[to], refs["bias_r"].at[me], {"dp": to}
        )

    for kind in (1, 0):
        for step in range(1, seqs):
            cut_copy(kind, lax.rem(me + step, seqs)).start()
    for step in range(1, seqs):
        bias_copy(lax.rem(me + step, seqs)).start()
    early = remote(
        refs["other"], early_out, refs["hand_s"].at[0], refs["hand_r"].at[0], {"section": ahead}
    )
    early.start()
    x[0, me, side] = cut[0, me]
    x[1, me, side] = cut[1, me]

    def fwd_copy(kind, b, half):
        return remote(
            x.at[kind, b, half], x.at[kind, b, half], refs["fwd_s"].at[kind, b],
            refs["fwd_r"].at[kind, b], {"seq": 1 - side},
        )

    def forward(b):
        @pl.when(b != me)
        def _():
            for kind in (1, 0):
                remote(
                    cut.at[kind, b], x.at[kind, b, side], refs["cut_s"].at[kind, b],
                    refs["cut_r"].at[kind, b], {"dp": b},
                ).wait_recv()
                fwd_copy(kind, b, side).start()

        @pl.when(b == me)
        def _():
            for kind in (1, 0):
                fwd_copy(kind, b, side).start()

    def part_copy(b, step):
        to = lax.rem(me + step, seqs)
        return remote(
            refs["part"].at[b, to], refs["got"].at[b, step - 1], refs["part_s"].at[b, step - 1],
            refs["part_r"].at[b, step - 1], {"dp": to},
        )

    def project(b):
        for kind in (1, 0):
            fwd_copy(kind, b, 1 - side).wait_recv()
        for step in list(range(1, seqs)) + [0]:
            to = lax.rem(me + step, seqs)
            at = pl.ds(pl.multiple_of(to * own, own), own)
            for which in range(3):
                product = jnp.dot(
                    x[min(which, 1), b].reshape(tokens, depth), weights[which, :, at],
                    preferred_element_type=F32,
                )
                if step:
                    refs["part"][b, to, which] = product.astype(BF16)
                else:
                    refs["mine"][b, which] = product
            if step:
                part_copy(b, step).start()

    def y_copy(b):
        return remote(
            refs["y_out"].at[b], refs["y_in"].at[b], refs["y_s"].at[b], refs["y_r"].at[b],
            {"seq": 1 - side},
        )

    def attend_one(b):
        for step in range(1, seqs):
            part_copy(b, step).wait_recv()

        @pl.when(b != me)
        def _():
            remote(
                bias.at[b], bias.at[b], refs["bias_s"].at[b], refs["bias_r"].at[b], {"dp": b}
            ).wait_recv()

        for which in range(3):
            total = refs["mine"][b, which]
            for step in range(seqs - 1):
                total += refs["got"][b, step, which].astype(F32)
            refs["qkv"][which] = total.astype(BF16)
        hide = bias[b][0:1, :]
        lane = lax.broadcasted_iota(jnp.int32, (1, LANES), 1)
        group = LANES // HEAD_DIM
        for pair in range(own // LANES):
            at = pl.ds(pair * LANES, LANES)
            query, key, value = (refs["qkv"][which, :, at] for which in range(3))
            result = None
            for h in range(group):
                inside = (lane >= h * HEAD_DIM) & (lane < (h + 1) * HEAD_DIM)
                scores = lax.dot_general(
                    jnp.where(inside, query, jnp.bfloat16(0.0)), key, (((1,), (1,)), ((), ())),
                    preferred_element_type=F32,
                ) * HEAD_DIM ** (-0.5) + hide
                raw = jnp.exp(scores - jnp.max(scores, axis=-1, keepdims=True))
                soft = (raw / jnp.sum(raw, axis=-1, keepdims=True)).astype(BF16)
                out = jnp.dot(soft, value, preferred_element_type=F32)
                result = out if result is None else jnp.where(inside, out, result)
            refs["heads"][:, at] = result.astype(BF16)
        heads = refs["heads"][...]
        for start in range(0, width, OUT_CHUNK):
            at = pl.ds(start, OUT_CHUNK)
            product = jnp.dot(heads, w_out[:, at], preferred_element_type=F32)
            low, high = product[:rows], product[rows:]
            refs["half"][b, :, at] = jnp.where(side == 0, low, high)
            refs["y_out"][b, :, at] = jnp.where(side == 0, high, low).astype(BF16)
        y_copy(b).start()

    def z_copy(b):
        return remote(
            refs["z_out"].at[b], refs["z_in"].at[me], refs["z_s"].at[b], refs["z_r"].at[me],
            {"dp": b},
        )

    def hand_over(b):
        y_copy(b).wait_recv()

        @pl.when(b != me)
        def _():
            refs["z_out"][b] = (refs["half"][b] + refs["y_in"][b].astype(F32)).astype(BF16)
            z_copy(b).start()

    forward(0)

    def turn(t, carry):
        @pl.when(t < seqs - 1)
        def _():
            forward(t + 1)

        @pl.when(t == 0)
        def _():
            for load in loads:
                load.wait()

        @pl.when(t < seqs)
        def _():
            project(t)

        @pl.when((t >= AHEAD) & (t < seqs + AHEAD))
        def _():
            attend_one(t - AHEAD)

        @pl.when(t >= AHEAD + 1)
        def _():
            hand_over(t - AHEAD - 1)

        return carry

    lax.fori_loop(0, seqs + AHEAD + 1, turn, 0)

    for step in range(1, seqs):
        b = lax.rem(me + step, seqs)
        remote(
            refs["z_out"].at[b], refs["z_in"].at[b], refs["z_s"].at[b], refs["z_r"].at[b],
            {"dp": b},
        ).wait_recv()

    def final_block(r, carry):
        at = pl.ds(pl.multiple_of(r * ROW_BLOCK, ROW_BLOCK), ROW_BLOCK)
        update = refs["half"][me, at, :] + refs["y_in"][me, at, :].astype(F32)
        for step in range(1, seqs):
            update += refs["z_in"][lax.rem(me + step, seqs), at, :].astype(F32)
        residual = residual_rows(at)
        place = side * rows + r * ROW_BLOCK + lax.broadcasted_iota(jnp.int32, (ROW_BLOCK, 1), 0)
        kept = jnp.where(place < tgt_len[0, 0], update, jnp.float32(0.0))
        decoded = (residual + kept).astype(BF16)
        encoded = normed(residual + update, last_gain[...])
        refs["late"][at, :] = jnp.where(is_first, encoded, decoded)
        return carry

    lax.fori_loop(0, rows // ROW_BLOCK, final_block, 0)
    late = remote(
        refs["late"], late_out, refs["hand_s"].at[1], refs["hand_r"].at[1], {"section": ahead}
    )
    late.start()

    for step in range(1, seqs):
        b = lax.rem(me + step, seqs)
        for kind in range(2):
            cut_copy(kind, b).wait_send()
        bias_copy(b).wait_send()
        z_copy(b).wait_send()

    def drain(b, carry):
        for kind in range(2):
            fwd_copy(kind, b, side).wait_send()
        for step in range(1, seqs):
            part_copy(b, step).wait_send()
        y_copy(b).wait_send()
        return carry

    lax.fori_loop(0, seqs, drain, 0)
    early.wait()
    late.wait()


def one_kernel(
    act_rows, mem_rows, w_query, w_key, w_value, w_out, ln_gain, final_gain, src_len, tgt_len
):
    rows, width = act_rows.shape[2:]
    depth, cols = w_query.shape[1:]
    seqs = lax.axis_size("dp")
    vmem, sems = scratch_of(seqs, rows, width, depth, cols)
    in_vmem = pl.BlockSpec(memory_space=pltpu.VMEM)
    in_hbm = pl.BlockSpec(memory_space=pl.ANY)
    in_smem = pl.BlockSpec(memory_space=pltpu.SMEM)
    out = jax.ShapeDtypeStruct((rows, width), BF16)
    total = 2 * rows * seqs
    early, late = pl.pallas_call(
        functools.partial(tick_kernel, tuple(vmem) + tuple(sems)),
        out_shape=(out, out),
        in_specs=[in_vmem] * 2 + [in_hbm] * 4 + [in_vmem] * 2 + [in_smem] * 2,
        out_specs=(in_vmem, in_vmem),
        scratch_shapes=[pltpu.VMEM(*spec) for spec in vmem.values()]
        + [pltpu.SemaphoreType.DMA(shape) for shape in sems.values()],
        compiler_params=pltpu.CompilerParams(
            collective_id=0, has_side_effects=True, vmem_limit_bytes=VMEM_BYTES
        ),
        cost_estimate=pl.CostEstimate(
            flops=8 * total * depth * cols, bytes_accessed=8 * depth * cols, transcendentals=0
        ),
    )(
        act_rows[0, 0], mem_rows[0, 0], w_query[0], w_key[0], w_value[0], w_out[0],
        ln_gain, final_gain[None], src_len, tgt_len,
    )
    from_first = lax.axis_index("section") == 1
    next_act = jnp.where(from_first, early, late)
    next_mem = jnp.where(from_first, late, early)
    return (next_act[None, None], next_mem[None, None])


def tick(*args):
    rows, width = args[0].shape[2:]
    depth, cols = args[2].shape[1:]
    if fits(lax.axis_size("dp"), lax.axis_size("seq"), rows, width, depth, cols):
        return one_kernel(*args)
    return per_device(*args)


def solution(mesh):
    return jax.shard_map(
        tick,
        mesh=mesh,
        in_specs=(
            P("section", "dp", "seq", None),
            P("section", "dp", "seq", None),
            P("section", "dp", "seq"),
            P("section", "dp", "seq"),
            P("section", "dp", "seq"),
            P("section", ("seq", "dp"), None),
            P("section", None),
            P(),
            P("section", "dp"),
            P("section", "dp"),
        ),
        out_specs=(P("section", "dp", "seq", None), P("section", "dp", "seq", None)),
        check_vma=False,
    )
```

```python
import functools

import jax
import jax.numpy as jnp
from jax import lax
from jax.experimental import pallas as pl
from jax.experimental.pallas import tpu as pltpu
from jax.sharding import PartitionSpec as P

HEAD_DIM = 64


EPS = 1e-06


def passed_along(x, axis, by):
    count = lax.axis_size(axis)
    return lax.ppermute(x, axis, [(i, (i + by) % count) for i in range(count)])


def normed(rows, gain):
    values = rows.astype(jnp.float32)
    scaled = values * lax.rsqrt(jnp.mean(values * values, axis=-1, keepdims=True) + EPS)
    return (scaled * gain).astype(jnp.bfloat16)


def attend(queries, keys, values, src_len):
    seqs, total_rows, width = queries.shape
    head_count = width // HEAD_DIM
    shape = (seqs, total_rows, head_count, HEAD_DIM)
    queries, keys, values = (a.reshape(shape) for a in (queries, keys, values))
    visible = jnp.arange(total_rows, dtype=jnp.int32)[None, :] < src_len[:, None]
    scores = jnp.einsum(
        "bqhd,bkhd->bhqk", queries, keys, preferred_element_type=jnp.float32
    ) * HEAD_DIM ** (-0.5)
    scores = jnp.where(visible[:, None, None, :], scores, -1e30)
    top_score = jnp.max(scores, axis=-1, keepdims=True)
    raw_weights = jnp.exp(scores - top_score)
    weights = (raw_weights / jnp.sum(raw_weights, axis=-1, keepdims=True)).astype(jnp.bfloat16)
    heads = jnp.einsum("bhqk,bkhd->bqhd", weights, values, preferred_element_type=jnp.float32)
    return heads.astype(jnp.bfloat16).reshape(seqs, total_rows, width)


def per_device(
    act_rows, mem_rows, w_query, w_key, w_value, w_out, ln_gain, final_gain, src_len, tgt_len
):
    is_first = lax.axis_index("section") == 0
    seqs = lax.axis_size("dp")
    halves = lax.axis_size("seq")
    act_here = act_rows[0, 0]
    mem_here = mem_rows[0, 0]
    rows_here, width = act_here.shape
    gain = ln_gain[0]
    depth, cols = w_query.shape[1:]
    own = cols // seqs
    rows_in = jnp.where(is_first, mem_here, act_here)
    query_in = normed(rows_in, gain)
    source_in = jnp.where(is_first, query_in, mem_here)
    both = jnp.stack([query_in, source_in]).reshape(2, rows_here, seqs, depth)
    both = lax.all_to_all(both.transpose(2, 0, 1, 3), "dp", 0, 0, tiled=True)
    both = lax.all_gather(both, "seq", axis=0, tiled=False)
    both = both.transpose(2, 1, 0, 3, 4).reshape(2, seqs * halves * rows_here, depth)
    total = seqs * halves * rows_here

    def project(rows, weight):
        part = jnp.dot(rows, weight[0], preferred_element_type=jnp.float32).astype(jnp.bfloat16)
        part = part.reshape(total, seqs, own).transpose(1, 0, 2)
        part = lax.psum_scatter(part, "dp", scatter_dimension=0, tiled=False)
        return part.reshape(seqs, halves * rows_here, own)

    queries = project(both[0], w_query)
    keys = project(both[1], w_key)
    values = project(both[1], w_value)
    lengths = lax.all_gather(src_len[0], "dp", axis=0, tiled=True)
    heads_out = attend(queries, keys, values, lengths)
    update = jnp.dot(
        heads_out.reshape(total, own), w_out[0], preferred_element_type=jnp.float32
    ).astype(jnp.bfloat16).reshape(seqs, halves, rows_here, width)
    update = lax.psum_scatter(update, "seq", scatter_dimension=1, tiled=False)
    update = lax.psum_scatter(update, "dp", scatter_dimension=0, tiled=False).astype(jnp.float32)
    residual = rows_in.astype(jnp.float32)
    positions = lax.axis_index("seq") * rows_here + jnp.arange(rows_here, dtype=jnp.int32)
    keep_rows = (positions < tgt_len[0, 0])[:, None]
    decoded = (residual + jnp.where(keep_rows, update, jnp.float32(0.0))).astype(jnp.bfloat16)
    encoded = normed(residual + update, final_gain)
    emit_act = jnp.where(is_first, act_here, decoded)
    emit_mem = jnp.where(is_first, encoded, mem_here)
    next_act, next_mem = passed_along((emit_act, emit_mem), "section", 1)
    return (next_act[None, None], next_mem[None, None])


ROW_BLOCK = 16
LANES = 128
AHEAD = 3
OUT_CHUNK = 1024
VMEM_BYTES = 60 * 1024 * 1024
BF16 = jnp.bfloat16
F32 = jnp.float32


def scratch_of(seqs, rows, width, depth, cols):
    own, tokens = cols // seqs, 2 * rows
    vmem = {
        "weights": ((3, depth, cols), BF16),
        "w_out": ((own, width), BF16),
        "cut": ((2, seqs, rows, depth), BF16),
        "x": ((2, seqs, 2, rows, depth), BF16),
        "bias": ((seqs, 8, tokens), F32),
        "other": ((rows, width), BF16),
        "part": ((seqs, seqs, 3, tokens, own), BF16),
        "mine": ((seqs, 3, tokens, own), F32),
        "got": ((seqs, 4, 3, tokens, own), BF16),
        "far_part": ((2, 3, tokens, own), F32),
        "qkv": ((3, tokens, own), BF16),
        "heads": ((tokens, own), BF16),
        "half": ((seqs, rows, width), F32),
        "y_out": ((seqs, width // OUT_CHUNK, rows, OUT_CHUNK), BF16),
        "y_in": ((seqs, width // OUT_CHUNK, rows, OUT_CHUNK), BF16),
        "z_out": ((seqs, width // OUT_CHUNK, rows, OUT_CHUNK), BF16),
        "z_in": ((seqs, width // OUT_CHUNK, rows, OUT_CHUNK), BF16),
        "late": ((rows, width), BF16),
    }
    sems = {
        "load": (4,),
        "cut_s": (2, seqs), "cut_r": (2, seqs),
        "fwd_s": (2, seqs), "fwd_r": (2, seqs),
        "bias_s": (seqs,), "bias_r": (seqs,),
        "part_s": (seqs, 3), "part_r": (seqs, 4),
        "y_s": (seqs, width // OUT_CHUNK), "y_r": (seqs, width // OUT_CHUNK),
        "z_s": (seqs, width // OUT_CHUNK), "z_r": (seqs, width // OUT_CHUNK),
        "hand_s": (2,), "hand_r": (2,),
    }
    return vmem, sems


def fits(seqs, halves, rows, width, depth, cols):
    own = cols // seqs
    if seqs != 4 or halves != 2 or rows % ROW_BLOCK or own % LANES or depth % LANES or width % OUT_CHUNK:
        return False
    vmem, _ = scratch_of(seqs, rows, width, depth, cols)
    total = 8 * rows * width * 2
    for shape, dtype in vmem.values():
        count = jnp.dtype(dtype).itemsize
        for extent in shape:
            count *= extent
        total += count
    return total <= VMEM_BYTES - 2 * 1024 * 1024


def tick_kernel(
    names, act, mem, w_q, w_k, w_v, w_o, gain, last_gain, src_len, tgt_len, early_out, late_out, *scratch
):
    refs = dict(zip(names, scratch))
    weights, w_out, cut, x, bias = (refs[n] for n in ("weights", "w_out", "cut", "x", "bias"))
    seqs, rows, depth = cut.shape[1:]
    width = act.shape[1]
    tokens = 2 * rows
    own = w_out.shape[0]
    sections = lax.axis_size("section")
    section = lax.axis_index("section")
    side = lax.axis_index("seq")
    me = lax.axis_index("dp")
    near = me + 1 - 2 * lax.rem(me, 2)
    mirror = seqs - 1 - me
    far = seqs - 1 - near
    at_end = 1 - lax.rem(lax.div(me + 1, 2), 2)
    is_first = section == 0
    ahead = lax.rem(section + 1, sections)
    behind = lax.rem(section + sections - 1, sections)

    def remote(source, target, send, recv, device):
        return pltpu.make_async_remote_copy(
            src_ref=source, dst_ref=target, send_sem=send, recv_sem=recv,
            device_id=device, device_id_type=pl.DeviceIdType.MESH,
        )

    barrier = pltpu.get_barrier_semaphore()
    for step in range(1, seqs):
        pl.semaphore_signal(
            barrier, inc=1, device_id={"dp": lax.rem(me + step, seqs)},
            device_id_type=pl.DeviceIdType.MESH,
        )
    for device in ({"seq": 1 - side}, {"section": ahead}, {"section": behind}):
        pl.semaphore_signal(barrier, inc=1, device_id=device, device_id_type=pl.DeviceIdType.MESH)

    loads = [
        pltpu.make_async_copy(w_q, weights.at[0], refs["load"].at[0]),
        pltpu.make_async_copy(w_k, weights.at[1], refs["load"].at[1]),
        pltpu.make_async_copy(w_v, weights.at[2], refs["load"].at[2]),
        pltpu.make_async_copy(w_o, w_out, refs["load"].at[3]),
    ]
    for load in loads:
        load.start()

    @pl.when(at_end == 1)
    def _():
        refs["z_in"][mirror] = jnp.zeros((width // OUT_CHUNK, rows, OUT_CHUNK), BF16)

        def clear(b, carry):
            refs["got"][b, 0] = jnp.zeros((3, tokens, own), BF16)
            return carry

        lax.fori_loop(0, seqs, clear, 0)

    def residual_rows(at):
        return jnp.where(is_first, mem[at, :], act[at, :]).astype(F32)

    def norm_block(r, carry):
        at = pl.ds(pl.multiple_of(r * ROW_BLOCK, ROW_BLOCK), ROW_BLOCK)
        query_in = normed(residual_rows(at), gain[...])
        source_in = jnp.where(is_first, query_in, mem[at, :])
        refs["other"][at, :] = jnp.where(is_first, act[at, :], mem[at, :])
        for j in range(seqs):
            cut[0, j, at, :] = query_in[:, j * depth:(j + 1) * depth]
            cut[1, j, at, :] = source_in[:, j * depth:(j + 1) * depth]
        return carry

    lax.fori_loop(0, rows // ROW_BLOCK, norm_block, 0)
    place = lax.broadcasted_iota(jnp.int32, (8, tokens), 1)
    bias[me] = jnp.where(place < src_len[0, 0], jnp.float32(0.0), jnp.float32(-1e30))
    pl.semaphore_wait(barrier, seqs + 2)

    def cut_copy(kind, to):
        return remote(
            cut.at[kind, to], x.at[kind, me, side], refs["cut_s"].at[kind, to],
            refs["cut_r"].at[kind, me], {"dp": to},
        )

    def bias_copy(to):
        return remote(
            bias.at[me], bias.at[me], refs["bias_s"].at[to], refs["bias_r"].at[me], {"dp": to}
        )

    for kind in (1, 0):
        for step in range(1, seqs):
            cut_copy(kind, lax.rem(me + step, seqs)).start()
    for step in range(1, seqs):
        bias_copy(lax.rem(me + step, seqs)).start()
    early = remote(
        refs["other"], early_out, refs["hand_s"].at[0], refs["hand_r"].at[0], {"section": ahead}
    )
    early.start()
    x[0, me, side] = cut[0, me]
    x[1, me, side] = cut[1, me]

    def fwd_copy(kind, b, half):
        return remote(
            x.at[kind, b, half], x.at[kind, b, half], refs["fwd_s"].at[kind, b],
            refs["fwd_r"].at[kind, b], {"seq": 1 - side},
        )

    def order(t):
        return lax.div(t + 3, 4) * (1 + lax.rem(t + 1, 3))

    def forward(b):
        @pl.when(b != me)
        def _():
            for kind in (1, 0):
                remote(
                    cut.at[kind, b], x.at[kind, b, side], refs["cut_s"].at[kind, b],
                    refs["cut_r"].at[kind, b], {"dp": b},
                ).wait_recv()
                fwd_copy(kind, b, side).start()

        @pl.when(b == me)
        def _():
            for kind in (1, 0):
                fwd_copy(kind, b, side).start()

    def part_copy(b, relation):
        if relation == 0:
            block, slot = mirror, 3 * at_end
            device = at_end * near + (1 - at_end) * mirror
        else:
            block, slot = (near, far)[relation - 1], relation
            device = block
        return remote(
            refs["part"].at[b, block], refs["got"].at[b, slot], refs["part_s"].at[b, relation],
            refs["part_r"].at[b, slot], {"dp": device},
        )

    def part_here(b, slot):
        return remote(
            refs["part"].at[b, near], refs["got"].at[b, slot], refs["part_s"].at[b, 1],
            refs["part_r"].at[b, slot], {"dp": near},
        )

    def project(t):
        b = order(t)
        for kind in (1, 0):
            fwd_copy(kind, b, 1 - side).wait_recv()
        for relation, to in enumerate((mirror, near, far, me)):
            at = pl.ds(pl.multiple_of(to * own, own), own)
            for which in range(3):
                product = jnp.dot(
                    x[min(which, 1), b].reshape(tokens, depth), weights[which, :, at],
                    preferred_element_type=F32,
                )
                if relation == 3:
                    refs["mine"][b, which] = product
                else:
                    refs["part"][b, to, which] = product.astype(BF16)
                if relation == 2:
                    refs["far_part"][lax.rem(t, 2), which] = product
            if relation < 2:
                part_copy(b, relation).start()
            elif relation == 2:
                @pl.when(at_end == 1)
                def _():
                    part_copy(b, 2).start()

    def merge(t):
        b = order(t)

        @pl.when(at_end == 0)
        def _():
            part_here(b, 3).wait_recv()
            for which in range(3):
                total = refs["far_part"][lax.rem(t, 2), which] + refs["got"][b, 3, which].astype(F32)
                refs["part"][b, far, which] = total.astype(BF16)
            part_copy(b, 2).start()

    chunks = width // OUT_CHUNK

    def y_copy(b, c):
        return remote(
            refs["y_out"].at[b, c], refs["y_in"].at[b, c], refs["y_s"].at[b, c],
            refs["y_r"].at[b, c], {"seq": 1 - side},
        )

    def attend_one(t):
        b = order(t)

        @pl.when(at_end == 0)
        def _():
            part_here(b, 0).wait_recv()

        part_here(b, 1).wait_recv()
        part_here(b, 2).wait_recv()

        @pl.when(b != me)
        def _():
            remote(
                bias.at[b], bias.at[b], refs["bias_s"].at[b], refs["bias_r"].at[b], {"dp": b}
            ).wait_recv()

        for which in range(3):
            total = refs["mine"][b, which]
            for step in range(seqs - 1):
                total += refs["got"][b, step, which].astype(F32)
            refs["qkv"][which] = total.astype(BF16)
        hide = bias[b][0:1, :]
        lane = lax.broadcasted_iota(jnp.int32, (1, LANES), 1)
        group = LANES // HEAD_DIM
        for pair in range(own // LANES):
            at = pl.ds(pair * LANES, LANES)
            query, key, value = (refs["qkv"][which, :, at] for which in range(3))
            result = None
            for h in range(group):
                inside = (lane >= h * HEAD_DIM) & (lane < (h + 1) * HEAD_DIM)
                scores = lax.dot_general(
                    jnp.where(inside, query, jnp.bfloat16(0.0)), key, (((1,), (1,)), ((), ())),
                    preferred_element_type=F32,
                ) * HEAD_DIM ** (-0.5) + hide
                raw = jnp.exp(scores - jnp.max(scores, axis=-1, keepdims=True))
                soft = (raw / jnp.sum(raw, axis=-1, keepdims=True)).astype(BF16)
                out = jnp.dot(soft, value, preferred_element_type=F32)
                result = out if result is None else jnp.where(inside, out, result)
            refs["heads"][:, at] = result.astype(BF16)
        heads = refs["heads"][...]
        for c in range(chunks):
            at = pl.ds(c * OUT_CHUNK, OUT_CHUNK)
            product = jnp.dot(heads, w_out[:, at], preferred_element_type=F32)
            low, high = product[:rows], product[rows:]
            refs["half"][b, :, at] = jnp.where(side == 0, low, high)
            refs["y_out"][b, c] = jnp.where(side == 0, high, low).astype(BF16)
            y_copy(b, c).start()

    def z_copy(b, c, device, slot):
        return remote(
            refs["z_out"].at[b, c], refs["z_in"].at[slot, c], refs["z_s"].at[b, c],
            refs["z_r"].at[slot, c], {"dp": device},
        )

    def hand_over(t):
        b = order(t)
        merged = (b == far) & (at_end == 0)
        passed = (b == mirror) & (at_end == 1)
        for c in range(chunks):
            at = pl.ds(c * OUT_CHUNK, OUT_CHUNK)
            y_copy(b, c).wait_recv()

            @pl.when((b != me) & jnp.logical_not(merged))
            def _():
                total = refs["half"][b, :, at] + refs["y_in"][b, c].astype(F32)
                refs["z_out"][b, c] = total.astype(BF16)

            @pl.when(merged)
            def _():
                z_copy(b, c, near, me).wait_recv()
                total = refs["half"][b, :, at] + refs["y_in"][b, c].astype(F32)
                refs["z_out"][b, c] = (total + refs["z_in"][me, c].astype(F32)).astype(BF16)

            @pl.when(passed)
            def _():
                z_copy(b, c, near, near).start()

            @pl.when((b != me) & jnp.logical_not(passed))
            def _():
                z_copy(b, c, b, me).start()

    forward(0)

    def turn(t, carry):
        @pl.when(t < seqs - 1)
        def _():
            forward(order(t + 1))

        @pl.when(t == 0)
        def _():
            for load in loads:
                load.wait()

        @pl.when(t < seqs)
        def _():
            project(t)

        @pl.when((t >= 1) & (t < seqs + 1))
        def _():
            merge(t - 1)

        @pl.when((t >= AHEAD) & (t < seqs + AHEAD))
        def _():
            attend_one(t - AHEAD)

        @pl.when(t >= AHEAD + 1)
        def _():
            hand_over(t - AHEAD - 1)

        return carry

    lax.fori_loop(0, seqs + AHEAD + 1, turn, 0)

    for c in range(chunks):
        z_copy(me, c, near, near).wait_recv()
        z_copy(me, c, far, far).wait_recv()

    @pl.when(at_end == 0)
    def _():
        for c in range(chunks):
            z_copy(me, c, mirror, mirror).wait_recv()

    def final_block(r, carry):
        at = pl.ds(pl.multiple_of(r * ROW_BLOCK, ROW_BLOCK), ROW_BLOCK)
        pieces = []
        for c in range(chunks):
            piece = refs["half"][me, at, c * OUT_CHUNK:(c + 1) * OUT_CHUNK]
            piece += refs["y_in"][me, c, at, :].astype(F32)
            for step in range(1, seqs):
                piece += refs["z_in"][lax.rem(me + step, seqs), c, at, :].astype(F32)
            pieces.append(piece)
        update = jnp.concatenate(pieces, axis=1)
        residual = residual_rows(at)
        place = side * rows + r * ROW_BLOCK + lax.broadcasted_iota(jnp.int32, (ROW_BLOCK, 1), 0)
        kept = jnp.where(place < tgt_len[0, 0], update, jnp.float32(0.0))
        decoded = (residual + kept).astype(BF16)
        encoded = normed(residual + update, last_gain[...])
        refs["late"][at, :] = jnp.where(is_first, encoded, decoded)
        return carry

    lax.fori_loop(0, rows // ROW_BLOCK, final_block, 0)
    late = remote(
        refs["late"], late_out, refs["hand_s"].at[1], refs["hand_r"].at[1], {"section": ahead}
    )
    late.start()

    for step in range(1, seqs):
        b = lax.rem(me + step, seqs)
        for kind in range(2):
            cut_copy(kind, b).wait_send()
        bias_copy(b).wait_send()
        for c in range(chunks):
            z_copy(b, c, b, me).wait_send()

    def drain(b, carry):
        for kind in range(2):
            fwd_copy(kind, b, side).wait_send()
        for relation in range(3):
            part_copy(b, relation).wait_send()
        for c in range(chunks):
            y_copy(b, c).wait_send()
        return carry

    lax.fori_loop(0, seqs, drain, 0)
    early.wait()
    late.wait()


def one_kernel(
    act_rows, mem_rows, w_query, w_key, w_value, w_out, ln_gain, final_gain, src_len, tgt_len
):
    rows, width = act_rows.shape[2:]
    depth, cols = w_query.shape[1:]
    seqs = lax.axis_size("dp")
    vmem, sems = scratch_of(seqs, rows, width, depth, cols)
    in_vmem = pl.BlockSpec(memory_space=pltpu.VMEM)
    in_hbm = pl.BlockSpec(memory_space=pl.ANY)
    in_smem = pl.BlockSpec(memory_space=pltpu.SMEM)
    out = jax.ShapeDtypeStruct((rows, width), BF16)
    total = 2 * rows * seqs
    early, late = pl.pallas_call(
        functools.partial(tick_kernel, tuple(vmem) + tuple(sems)),
        out_shape=(out, out),
        in_specs=[in_vmem] * 2 + [in_hbm] * 4 + [in_vmem] * 2 + [in_smem] * 2,
        out_specs=(in_vmem, in_vmem),
        scratch_shapes=[pltpu.VMEM(*spec) for spec in vmem.values()]
        + [pltpu.SemaphoreType.DMA(shape) for shape in sems.values()],
        compiler_params=pltpu.CompilerParams(
            collective_id=0, has_side_effects=True, vmem_limit_bytes=VMEM_BYTES
        ),
        cost_estimate=pl.CostEstimate(
            flops=8 * total * depth * cols, bytes_accessed=8 * depth * cols, transcendentals=0
        ),
    )(
        act_rows[0, 0], mem_rows[0, 0], w_query[0], w_key[0], w_value[0], w_out[0],
        ln_gain, final_gain[None], src_len, tgt_len,
    )
    from_first = lax.axis_index("section") == 1
    next_act = jnp.where(from_first, early, late)
    next_mem = jnp.where(from_first, late, early)
    return (next_act[None, None], next_mem[None, None])


def tick(*args):
    rows, width = args[0].shape[2:]
    depth, cols = args[2].shape[1:]
    if fits(lax.axis_size("dp"), lax.axis_size("seq"), rows, width, depth, cols):
        return one_kernel(*args)
    return per_device(*args)


def solution(mesh):
    return jax.shard_map(
        tick,
        mesh=mesh,
        in_specs=(
            P("section", "dp", "seq", None),
            P("section", "dp", "seq", None),
            P("section", "dp", "seq"),
            P("section", "dp", "seq"),
            P("section", "dp", "seq"),
            P("section", ("seq", "dp"), None),
            P("section", None),
            P(),
            P("section", "dp"),
            P("section", "dp"),
        ),
        out_specs=(P("section", "dp", "seq", None), P("section", "dp", "seq", None)),
        check_vma=False,
    )
```

```python
import functools

import jax
import jax.numpy as jnp
from jax import lax
from jax.experimental import pallas as pl
from jax.experimental.pallas import tpu as pltpu
from jax.sharding import PartitionSpec as P

HEAD_DIM = 64


EPS = 1e-06


def passed_along(x, axis, by):
    count = lax.axis_size(axis)
    return lax.ppermute(x, axis, [(i, (i + by) % count) for i in range(count)])


def normed(rows, gain):
    values = rows.astype(jnp.float32)
    scaled = values * lax.rsqrt(jnp.mean(values * values, axis=-1, keepdims=True) + EPS)
    return (scaled * gain).astype(jnp.bfloat16)


def attend(queries, keys, values, src_len):
    seqs, total_rows, width = queries.shape
    head_count = width // HEAD_DIM
    shape = (seqs, total_rows, head_count, HEAD_DIM)
    queries, keys, values = (a.reshape(shape) for a in (queries, keys, values))
    visible = jnp.arange(total_rows, dtype=jnp.int32)[None, :] < src_len[:, None]
    scores = jnp.einsum(
        "bqhd,bkhd->bhqk", queries, keys, preferred_element_type=jnp.float32
    ) * HEAD_DIM ** (-0.5)
    scores = jnp.where(visible[:, None, None, :], scores, -1e30)
    top_score = jnp.max(scores, axis=-1, keepdims=True)
    raw_weights = jnp.exp(scores - top_score)
    weights = (raw_weights / jnp.sum(raw_weights, axis=-1, keepdims=True)).astype(jnp.bfloat16)
    heads = jnp.einsum("bhqk,bkhd->bqhd", weights, values, preferred_element_type=jnp.float32)
    return heads.astype(jnp.bfloat16).reshape(seqs, total_rows, width)


def per_device(
    act_rows, mem_rows, w_query, w_key, w_value, w_out, ln_gain, final_gain, src_len, tgt_len
):
    is_first = lax.axis_index("section") == 0
    seqs = lax.axis_size("dp")
    halves = lax.axis_size("seq")
    act_here = act_rows[0, 0]
    mem_here = mem_rows[0, 0]
    rows_here, width = act_here.shape
    gain = ln_gain[0]
    depth, cols = w_query.shape[1:]
    own = cols // seqs
    rows_in = jnp.where(is_first, mem_here, act_here)
    query_in = normed(rows_in, gain)
    source_in = jnp.where(is_first, query_in, mem_here)
    both = jnp.stack([query_in, source_in]).reshape(2, rows_here, seqs, depth)
    both = lax.all_to_all(both.transpose(2, 0, 1, 3), "dp", 0, 0, tiled=True)
    both = lax.all_gather(both, "seq", axis=0, tiled=False)
    both = both.transpose(2, 1, 0, 3, 4).reshape(2, seqs * halves * rows_here, depth)
    total = seqs * halves * rows_here

    def project(rows, weight):
        part = jnp.dot(rows, weight[0], preferred_element_type=jnp.float32).astype(jnp.bfloat16)
        part = part.reshape(total, seqs, own).transpose(1, 0, 2)
        part = lax.psum_scatter(part, "dp", scatter_dimension=0, tiled=False)
        return part.reshape(seqs, halves * rows_here, own)

    queries = project(both[0], w_query)
    keys = project(both[1], w_key)
    values = project(both[1], w_value)
    lengths = lax.all_gather(src_len[0], "dp", axis=0, tiled=True)
    heads_out = attend(queries, keys, values, lengths)
    update = jnp.dot(
        heads_out.reshape(total, own), w_out[0], preferred_element_type=jnp.float32
    ).astype(jnp.bfloat16).reshape(seqs, halves, rows_here, width)
    update = lax.psum_scatter(update, "seq", scatter_dimension=1, tiled=False)
    update = lax.psum_scatter(update, "dp", scatter_dimension=0, tiled=False).astype(jnp.float32)
    residual = rows_in.astype(jnp.float32)
    positions = lax.axis_index("seq") * rows_here + jnp.arange(rows_here, dtype=jnp.int32)
    keep_rows = (positions < tgt_len[0, 0])[:, None]
    decoded = (residual + jnp.where(keep_rows, update, jnp.float32(0.0))).astype(jnp.bfloat16)
    encoded = normed(residual + update, final_gain)
    emit_act = jnp.where(is_first, act_here, decoded)
    emit_mem = jnp.where(is_first, encoded, mem_here)
    next_act, next_mem = passed_along((emit_act, emit_mem), "section", 1)
    return (next_act[None, None], next_mem[None, None])


ROW_BLOCK = 16
LANES = 128
AHEAD = 3
OUT_CHUNK = 512
VMEM_BYTES = 60 * 1024 * 1024
BF16 = jnp.bfloat16
F32 = jnp.float32


def scratch_of(seqs, rows, width, depth, cols):
    own, tokens = cols // seqs, 2 * rows
    vmem = {
        "weights": ((3, depth, cols), BF16),
        "w_out": ((own, width), BF16),
        "cut": ((2, seqs, rows, depth), BF16),
        "x": ((2, seqs, 2, rows, depth), BF16),
        "bias": ((seqs, 8, tokens), F32),
        "other": ((rows, width), BF16),
        "part": ((seqs, seqs, 3, tokens, own), BF16),
        "mine": ((seqs, 3, tokens, own), F32),
        "got": ((seqs, 4, 3, tokens, own), BF16),
        "far_part": ((2, 3, tokens, own), F32),
        "qkv": ((3, tokens, own), BF16),
        "heads": ((tokens, own), BF16),
        "half": ((seqs, rows, width), F32),
        "y_out": ((seqs, width // OUT_CHUNK, rows, OUT_CHUNK), BF16),
        "y_in": ((seqs, width // OUT_CHUNK, rows, OUT_CHUNK), BF16),
        "z_out": ((seqs, width // OUT_CHUNK, rows, OUT_CHUNK), BF16),
        "z_in": ((seqs, width // OUT_CHUNK, rows, OUT_CHUNK), BF16),
        "late": ((rows, width), BF16),
    }
    sems = {
        "load": (4,),
        "cut_s": (2, seqs), "cut_r": (2, seqs),
        "fwd_s": (2, seqs), "fwd_r": (2, seqs),
        "bias_s": (seqs,), "bias_r": (seqs,),
        "part_s": (seqs, 3), "part_r": (seqs, 4),
        "y_s": (seqs, width // OUT_CHUNK), "y_r": (seqs, width // OUT_CHUNK),
        "z_s": (seqs, width // OUT_CHUNK), "z_r": (seqs, width // OUT_CHUNK),
        "hand_s": (2,), "hand_r": (2,),
    }
    return vmem, sems


def fits(seqs, halves, rows, width, depth, cols):
    own = cols // seqs
    if seqs != 4 or halves != 2 or rows % ROW_BLOCK or own % LANES or depth % LANES or width % OUT_CHUNK:
        return False
    vmem, _ = scratch_of(seqs, rows, width, depth, cols)
    total = 8 * rows * width * 2
    for shape, dtype in vmem.values():
        count = jnp.dtype(dtype).itemsize
        for extent in shape:
            count *= extent
        total += count
    return total <= VMEM_BYTES - 2 * 1024 * 1024


def tick_kernel(
    names, act, mem, w_q, w_k, w_v, w_o, gain, last_gain, src_len, tgt_len, early_out, late_out, *scratch
):
    refs = dict(zip(names, scratch))
    weights, w_out, cut, x, bias = (refs[n] for n in ("weights", "w_out", "cut", "x", "bias"))
    seqs, rows, depth = cut.shape[1:]
    width = act.shape[1]
    tokens = 2 * rows
    own = w_out.shape[0]
    sections = lax.axis_size("section")
    section = lax.axis_index("section")
    side = lax.axis_index("seq")
    me = lax.axis_index("dp")
    near = me + 1 - 2 * lax.rem(me, 2)
    mirror = seqs - 1 - me
    far = seqs - 1 - near
    at_end = 1 - lax.rem(lax.div(me + 1, 2), 2)
    is_first = section == 0
    ahead = lax.rem(section + 1, sections)
    behind = lax.rem(section + sections - 1, sections)

    def remote(source, target, send, recv, device):
        return pltpu.make_async_remote_copy(
            src_ref=source, dst_ref=target, send_sem=send, recv_sem=recv,
            device_id=device, device_id_type=pl.DeviceIdType.MESH,
        )

    barrier = pltpu.get_barrier_semaphore()
    for step in range(1, seqs):
        pl.semaphore_signal(
            barrier, inc=1, device_id={"dp": lax.rem(me + step, seqs)},
            device_id_type=pl.DeviceIdType.MESH,
        )
    for device in ({"seq": 1 - side}, {"section": ahead}, {"section": behind}):
        pl.semaphore_signal(barrier, inc=1, device_id=device, device_id_type=pl.DeviceIdType.MESH)

    loads = [
        pltpu.make_async_copy(w_q, weights.at[0], refs["load"].at[0]),
        pltpu.make_async_copy(w_k, weights.at[1], refs["load"].at[1]),
        pltpu.make_async_copy(w_v, weights.at[2], refs["load"].at[2]),
        pltpu.make_async_copy(w_o, w_out, refs["load"].at[3]),
    ]
    for load in loads:
        load.start()

    @pl.when(at_end == 1)
    def _():
        refs["z_in"][mirror] = jnp.zeros((width // OUT_CHUNK, rows, OUT_CHUNK), BF16)

        def clear(b, carry):
            refs["got"][b, 0] = jnp.zeros((3, tokens, own), BF16)
            return carry

        lax.fori_loop(0, seqs, clear, 0)

    def residual_rows(at):
        return jnp.where(is_first, mem[at, :], act[at, :]).astype(F32)

    def norm_block(r, carry):
        at = pl.ds(pl.multiple_of(r * ROW_BLOCK, ROW_BLOCK), ROW_BLOCK)
        query_in = normed(residual_rows(at), gain[...])
        source_in = jnp.where(is_first, query_in, mem[at, :])
        refs["other"][at, :] = jnp.where(is_first, act[at, :], mem[at, :])
        for j in range(seqs):
            cut[0, j, at, :] = query_in[:, j * depth:(j + 1) * depth]
            cut[1, j, at, :] = source_in[:, j * depth:(j + 1) * depth]
        return carry

    lax.fori_loop(0, rows // ROW_BLOCK, norm_block, 0)
    place = lax.broadcasted_iota(jnp.int32, (8, tokens), 1)
    bias[me] = jnp.where(place < src_len[0, 0], jnp.float32(0.0), jnp.float32(-1e30))
    pl.semaphore_wait(barrier, seqs + 2)

    def cut_copy(kind, to):
        return remote(
            cut.at[kind, to], x.at[kind, me, side], refs["cut_s"].at[kind, to],
            refs["cut_r"].at[kind, me], {"dp": to},
        )

    def bias_copy(to):
        return remote(
            bias.at[me], bias.at[me], refs["bias_s"].at[to], refs["bias_r"].at[me], {"dp": to}
        )

    for kind in (1, 0):
        for step in range(1, seqs):
            cut_copy(kind, lax.rem(me + step, seqs)).start()
    for step in range(1, seqs):
        bias_copy(lax.rem(me + step, seqs)).start()
    early = remote(
        refs["other"], early_out, refs["hand_s"].at[0], refs["hand_r"].at[0], {"section": ahead}
    )
    early.start()
    x[0, me, side] = cut[0, me]
    x[1, me, side] = cut[1, me]

    def fwd_copy(kind, b, half):
        return remote(
            x.at[kind, b, half], x.at[kind, b, half], refs["fwd_s"].at[kind, b],
            refs["fwd_r"].at[kind, b], {"seq": 1 - side},
        )

    def order(t):
        return lax.div(t + 3, 4) * (1 + lax.rem(t + 1, 3))

    def forward(b):
        @pl.when(b != me)
        def _():
            for kind in (1, 0):
                remote(
                    cut.at[kind, b], x.at[kind, b, side], refs["cut_s"].at[kind, b],
                    refs["cut_r"].at[kind, b], {"dp": b},
                ).wait_recv()
                fwd_copy(kind, b, side).start()

        @pl.when(b == me)
        def _():
            for kind in (1, 0):
                fwd_copy(kind, b, side).start()

    def part_copy(b, relation):
        if relation == 0:
            block, slot = mirror, 3 * at_end
            device = at_end * near + (1 - at_end) * mirror
        else:
            block, slot = (near, far)[relation - 1], relation
            device = block
        return remote(
            refs["part"].at[b, block], refs["got"].at[b, slot], refs["part_s"].at[b, relation],
            refs["part_r"].at[b, slot], {"dp": device},
        )

    def part_here(b, slot):
        return remote(
            refs["part"].at[b, near], refs["got"].at[b, slot], refs["part_s"].at[b, 1],
            refs["part_r"].at[b, slot], {"dp": near},
        )

    def project(t):
        b = order(t)
        for kind in (1, 0):
            fwd_copy(kind, b, 1 - side).wait_recv()
        for relation, to in enumerate((mirror, near, far, me)):
            at = pl.ds(pl.multiple_of(to * own, own), own)
            for which in range(3):
                product = jnp.dot(
                    x[min(which, 1), b].reshape(tokens, depth), weights[which, :, at],
                    preferred_element_type=F32,
                )
                if relation == 3:
                    refs["mine"][b, which] = product
                else:
                    refs["part"][b, to, which] = product.astype(BF16)
                if relation == 2:
                    refs["far_part"][lax.rem(t, 2), which] = product
            if relation < 2:
                part_copy(b, relation).start()
            elif relation == 2:
                @pl.when(at_end == 1)
                def _():
                    part_copy(b, 2).start()

    def merge(t):
        b = order(t)

        @pl.when(at_end == 0)
        def _():
            part_here(b, 3).wait_recv()
            for which in range(3):
                total = refs["far_part"][lax.rem(t, 2), which] + refs["got"][b, 3, which].astype(F32)
                refs["part"][b, far, which] = total.astype(BF16)
            part_copy(b, 2).start()

    chunks = width // OUT_CHUNK

    def y_copy(b, c):
        return remote(
            refs["y_out"].at[b, c], refs["y_in"].at[b, c], refs["y_s"].at[b, c],
            refs["y_r"].at[b, c], {"seq": 1 - side},
        )

    def attend_one(t):
        b = order(t)

        @pl.when(at_end == 0)
        def _():
            part_here(b, 0).wait_recv()

        part_here(b, 1).wait_recv()
        part_here(b, 2).wait_recv()

        @pl.when(b != me)
        def _():
            remote(
                bias.at[b], bias.at[b], refs["bias_s"].at[b], refs["bias_r"].at[b], {"dp": b}
            ).wait_recv()

        for which in range(3):
            total = refs["mine"][b, which]
            for step in range(seqs - 1):
                total += refs["got"][b, step, which].astype(F32)
            refs["qkv"][which] = total.astype(BF16)
        hide = bias[b][0:1, :]
        lane = lax.broadcasted_iota(jnp.int32, (1, LANES), 1)
        group = LANES // HEAD_DIM
        for pair in range(own // LANES):
            at = pl.ds(pair * LANES, LANES)
            query, key, value = (refs["qkv"][which, :, at] for which in range(3))
            result = None
            for h in range(group):
                inside = (lane >= h * HEAD_DIM) & (lane < (h + 1) * HEAD_DIM)
                scores = lax.dot_general(
                    jnp.where(inside, query, jnp.bfloat16(0.0)), key, (((1,), (1,)), ((), ())),
                    preferred_element_type=F32,
                ) * HEAD_DIM ** (-0.5) + hide
                raw = jnp.exp(scores - jnp.max(scores, axis=-1, keepdims=True))
                soft = (raw / jnp.sum(raw, axis=-1, keepdims=True)).astype(BF16)
                out = jnp.dot(soft, value, preferred_element_type=F32)
                result = out if result is None else jnp.where(inside, out, result)
            refs["heads"][:, at] = result.astype(BF16)
        heads = refs["heads"][...]
        for c in range(chunks):
            at = pl.ds(c * OUT_CHUNK, OUT_CHUNK)
            product = jnp.dot(heads, w_out[:, at], preferred_element_type=F32)
            low, high = product[:rows], product[rows:]
            refs["half"][b, :, at] = jnp.where(side == 0, low, high)
            refs["y_out"][b, c] = jnp.where(side == 0, high, low).astype(BF16)
            y_copy(b, c).start()

    def z_copy(b, c, device, slot):
        return remote(
            refs["z_out"].at[b, c], refs["z_in"].at[slot, c], refs["z_s"].at[b, c],
            refs["z_r"].at[slot, c], {"dp": device},
        )

    def hand_over(t):
        b = order(t)
        merged = (b == far) & (at_end == 0)
        passed = (b == mirror) & (at_end == 1)
        for c in range(chunks):
            at = pl.ds(c * OUT_CHUNK, OUT_CHUNK)
            y_copy(b, c).wait_recv()

            @pl.when((b != me) & jnp.logical_not(merged))
            def _():
                total = refs["half"][b, :, at] + refs["y_in"][b, c].astype(F32)
                refs["z_out"][b, c] = total.astype(BF16)

            @pl.when(merged)
            def _():
                z_copy(b, c, near, me).wait_recv()
                total = refs["half"][b, :, at] + refs["y_in"][b, c].astype(F32)
                refs["z_out"][b, c] = (total + refs["z_in"][me, c].astype(F32)).astype(BF16)

            @pl.when(passed)
            def _():
                z_copy(b, c, near, near).start()

            @pl.when((b != me) & jnp.logical_not(passed))
            def _():
                z_copy(b, c, b, me).start()

    forward(0)

    def turn(t, carry):
        @pl.when(t < seqs - 1)
        def _():
            forward(order(t + 1))

        @pl.when(t == 0)
        def _():
            for load in loads:
                load.wait()

        @pl.when(t < seqs)
        def _():
            project(t)

        @pl.when((t >= 1) & (t < seqs + 1))
        def _():
            merge(t - 1)

        @pl.when((t >= AHEAD) & (t < seqs + AHEAD))
        def _():
            attend_one(t - AHEAD)

        @pl.when(t >= AHEAD + 1)
        def _():
            hand_over(t - AHEAD - 1)

        return carry

    lax.fori_loop(0, seqs + AHEAD + 1, turn, 0)

    for c in range(chunks):
        z_copy(me, c, near, near).wait_recv()
        z_copy(me, c, far, far).wait_recv()

    @pl.when(at_end == 0)
    def _():
        for c in range(chunks):
            z_copy(me, c, mirror, mirror).wait_recv()

    def final_block(r, carry):
        at = pl.ds(pl.multiple_of(r * ROW_BLOCK, ROW_BLOCK), ROW_BLOCK)
        pieces = []
        for c in range(chunks):
            piece = refs["half"][me, at, c * OUT_CHUNK:(c + 1) * OUT_CHUNK]
            piece += refs["y_in"][me, c, at, :].astype(F32)
            for step in range(1, seqs):
                piece += refs["z_in"][lax.rem(me + step, seqs), c, at, :].astype(F32)
            pieces.append(piece)
        update = jnp.concatenate(pieces, axis=1)
        residual = residual_rows(at)
        place = side * rows + r * ROW_BLOCK + lax.broadcasted_iota(jnp.int32, (ROW_BLOCK, 1), 0)
        kept = jnp.where(place < tgt_len[0, 0], update, jnp.float32(0.0))
        decoded = (residual + kept).astype(BF16)
        encoded = normed(residual + update, last_gain[...])
        refs["late"][at, :] = jnp.where(is_first, encoded, decoded)
        return carry

    lax.fori_loop(0, rows // ROW_BLOCK, final_block, 0)
    late = remote(
        refs["late"], late_out, refs["hand_s"].at[1], refs["hand_r"].at[1], {"section": ahead}
    )
    late.start()

    for step in range(1, seqs):
        b = lax.rem(me + step, seqs)
        for kind in range(2):
            cut_copy(kind, b).wait_send()
        bias_copy(b).wait_send()
        for c in range(chunks):
            z_copy(b, c, b, me).wait_send()

    def drain(b, carry):
        for kind in range(2):
            fwd_copy(kind, b, side).wait_send()
        for relation in range(3):
            part_copy(b, relation).wait_send()
        for c in range(chunks):
            y_copy(b, c).wait_send()
        return carry

    lax.fori_loop(0, seqs, drain, 0)
    early.wait()
    late.wait()


def one_kernel(
    act_rows, mem_rows, w_query, w_key, w_value, w_out, ln_gain, final_gain, src_len, tgt_len
):
    rows, width = act_rows.shape[2:]
    depth, cols = w_query.shape[1:]
    seqs = lax.axis_size("dp")
    vmem, sems = scratch_of(seqs, rows, width, depth, cols)
    in_vmem = pl.BlockSpec(memory_space=pltpu.VMEM)
    in_hbm = pl.BlockSpec(memory_space=pl.ANY)
    in_smem = pl.BlockSpec(memory_space=pltpu.SMEM)
    out = jax.ShapeDtypeStruct((rows, width), BF16)
    total = 2 * rows * seqs
    early, late = pl.pallas_call(
        functools.partial(tick_kernel, tuple(vmem) + tuple(sems)),
        out_shape=(out, out),
        in_specs=[in_vmem] * 2 + [in_hbm] * 4 + [in_vmem] * 2 + [in_smem] * 2,
        out_specs=(in_vmem, in_vmem),
        scratch_shapes=[pltpu.VMEM(*spec) for spec in vmem.values()]
        + [pltpu.SemaphoreType.DMA(shape) for shape in sems.values()],
        compiler_params=pltpu.CompilerParams(
            collective_id=0, has_side_effects=True, vmem_limit_bytes=VMEM_BYTES
        ),
        cost_estimate=pl.CostEstimate(
            flops=8 * total * depth * cols, bytes_accessed=8 * depth * cols, transcendentals=0
        ),
    )(
        act_rows[0, 0], mem_rows[0, 0], w_query[0], w_key[0], w_value[0], w_out[0],
        ln_gain, final_gain[None], src_len, tgt_len,
    )
    from_first = lax.axis_index("section") == 1
    next_act = jnp.where(from_first, early, late)
    next_mem = jnp.where(from_first, late, early)
    return (next_act[None, None], next_mem[None, None])


def tick(*args):
    rows, width = args[0].shape[2:]
    depth, cols = args[2].shape[1:]
    if fits(lax.axis_size("dp"), lax.axis_size("seq"), rows, width, depth, cols):
        return one_kernel(*args)
    return per_device(*args)


def solution(mesh):
    return jax.shard_map(
        tick,
        mesh=mesh,
        in_specs=(
            P("section", "dp", "seq", None),
            P("section", "dp", "seq", None),
            P("section", "dp", "seq"),
            P("section", "dp", "seq"),
            P("section", "dp", "seq"),
            P("section", ("seq", "dp"), None),
            P("section", None),
            P(),
            P("section", "dp"),
            P("section", "dp"),
        ),
        out_specs=(P("section", "dp", "seq", None), P("section", "dp", "seq", None)),
        check_vma=False,
    )
```
